512 devices in a mesh: ctx: 64 (over y_lo, z, core), head: 8 (over y_hi, x).
Axes of the slice: x: 4, y: 8 (y_hi: 2, y_lo: 4; y = y_hi * 4 + y_lo), z: 8, core: 2. Of those that a mesh axis runs over, the one named last changes fastest.
Arguments:
- teacher_query: bfloat16 [8192, 8192], P('ctx', 'head'), may hold values from -6 to 6
- teacher_key: bfloat16 [8192, 1024], P('ctx', 'head'), may hold values from -6 to 6
- teacher_value: bfloat16 [8192, 1024], P('ctx', 'head'), may hold values from -6 to 6
- student_hidden: bfloat16 [8192, 4096], P(('ctx', 'head')), may hold values from -6 to 6
- weight_codes: int32 [4096, 2048], P('ctx', 'head'), may hold values from -8 to 7
- scale_exponents: int32 [2048], P('head'), may hold values from 1 to 3
Outputs:
- teacher_context: bfloat16 [8192, 8192], P('ctx', 'head')
- student_out: bfloat16 [8192, 2048], P(('ctx', 'head'))
- weight_grad: float32 [4096, 2048], P('ctx', 'head')
The draws below stay inside these ranges and needn't reach their ends.
All inputs are finite; a program needn't handle non-finite values.
Results may differ from the reference program's by a relative error of at most 0.0055.
Values may be sent and summed in bfloat16 or wider, within the bound.
No kernel may reach another device: no remote copies, remote signals or barrier semaphores. Data moves between devices by JAX's collectives and lax.ppermute only.
A program may use at most 64 MiB of HBM per device.

```python
import math
import jax
import jax.numpy as jnp
from jax import lax

TOK_DEV = 128
HEADS = 64
KV_HEADS = 8
HD = 128
D_S = 4096
S_HEADS = 16
TOKENS = 8192
POOL = 4


def draw_teacher_query(key, part):
    key = jax.random.fold_in(key, 3)
    first_key = jax.random.fold_in(key, 0)
    values = jnp.clip(1.6 * jax.random.normal(first_key, (TOKENS, HEADS, HD), jnp.float32), -6.0, 6.0)
    return values.reshape(TOKENS, HEADS * HD).astype(jnp.bfloat16)


def draw_teacher_key(key, part):
    key = jax.random.fold_in(key, 7)
    first_key = jax.random.fold_in(key, 0)
    values = jnp.clip(1.6 * jax.random.normal(first_key, (TOKENS, KV_HEADS, HD), jnp.float32), -6.0, 6.0)
    return values.reshape(TOKENS, KV_HEADS * HD).astype(jnp.bfloat16)


def place_ends(result, own_key, least, top_value):
    spot = [jax.random.randint(jax.random.fold_in(own_key, axis), (), 0, length) for axis, length in enumerate(result.shape)]
    main_axis = result.shape.index(max(result.shape))
    neighbour = spot[:main_axis] + [(spot[main_axis] + 1) % result.shape[main_axis]] + spot[main_axis + 1:]
    return result.at[tuple(spot)].set(least).at[tuple(neighbour)].set(top_value)


def steps_of(own_key, shape, cuts, low, largest):
    factor_of = 1.0
    for dim, shards_of in cuts:
        heights = jax.random.uniform(jax.random.fold_in(jax.random.fold_in(own_key, 6), dim), (shards_of,), jnp.float32, low / len(cuts), largest / len(cuts))
        factor_of = factor_of * jnp.repeat(jnp.exp(heights), shape[dim] // shards_of).reshape((-1,) + (1,) * (len(shape) - 1 - dim))
    return factor_of


def centred(stream_key, shape, scale, limit, pieces=(), held_as=jnp.bfloat16):
    gain = steps_of(stream_key, shape, pieces, -0.22, 0.18) if pieces else 1.0
    drawn = jax.random.normal(stream_key, shape, jnp.float32) * scale * gain
    return jnp.minimum(jnp.maximum(drawn, -limit), limit).astype(held_as)


def setup_inputs(seed: int = 0) -> dict:
    seeds = jax.random.split(jax.random.key(seed), 7)
    teacher_query = draw_teacher_query(jax.random.fold_in(seeds[6], 71), 0)
    teacher_key = draw_teacher_key(jax.random.fold_in(seeds[6], 71), 0)
    teacher_value = centred(seeds[2], (TOKENS, KV_HEADS * HD), 1.0, 6.0, ((0, 64), (1, 8)))
    student_hidden = centred(seeds[3], (TOKENS, D_S), 1.0, 6.0, ((0, 512),))
    weight_codes = place_ends(jax.random.randint(seeds[4], (D_S, S_HEADS * HD), -8, 8), jax.random.fold_in(seeds[4], 1), -8, 7).astype(jnp.int32)
    scale_exponents = place_ends(jax.random.randint(seeds[5], (S_HEADS * HD,), 1, 4), jax.random.fold_in(seeds[5], 1), 1, 3).astype(jnp.int32)
    return {"teacher_query": teacher_query, "teacher_key": teacher_key, "teacher_value": teacher_value, "student_hidden": student_hidden, "weight_codes": weight_codes, "scale_exponents": scale_exponents}


def reference(teacher_query, teacher_key, teacher_value, student_hidden, weight_codes, scale_exponents):
    group_size = HEADS // KV_HEADS
    score_scale = 1.0 / math.sqrt(HD)
    query_head_count = teacher_query.reshape(TOKENS, HEADS, HD)
    key_heads = teacher_key.reshape(TOKENS, KV_HEADS, HD)
    value_heads = teacher_value.reshape(TOKENS, KV_HEADS, HD)
    positions = jnp.arange(TOKENS, dtype=jnp.int32)

    def one_head(head_index):
        query_one = lax.dynamic_index_in_dim(query_head_count, head_index, 1, keepdims=False)
        key_one = lax.dynamic_index_in_dim(key_heads, head_index // group_size, 1, keepdims=False)
        value_one = lax.dynamic_index_in_dim(value_heads, head_index // group_size, 1, keepdims=False)

        def one_block(block_number):
            row_first = block_number * TOK_DEV
            query_rows = lax.dynamic_slice_in_dim(query_one, row_first, TOK_DEV, 0)
            scores = jnp.dot(query_rows, key_one.T, preferred_element_type=jnp.float32) * score_scale
            row_position = row_first + jnp.arange(TOK_DEV, dtype=jnp.int32)
            allowed = positions[None, :] <= row_position[:, None]
            scores = jnp.where(allowed, scores, -jnp.inf)
            row_top = lax.optimization_barrier(jnp.max(scores, axis=1, keepdims=True))
            probabilities = jnp.exp(scores - row_top)
            denominator = lax.optimization_barrier(jnp.sum(probabilities, axis=1, keepdims=True))
            summed = jnp.dot(probabilities.astype(jnp.bfloat16), value_one, preferred_element_type=jnp.float32)
            return (summed / denominator).astype(jnp.bfloat16)
        return lax.map(one_block, jnp.arange(TOKENS // TOK_DEV, dtype=jnp.int32))
    head_outputs = lax.map(one_head, jnp.arange(HEADS, dtype=jnp.int32))
    teacher_context = jnp.transpose(head_outputs.reshape(HEADS, TOKENS, HD), (1, 0, 2)).reshape(TOKENS, HEADS * HD)
    target = teacher_context.astype(jnp.float32).reshape(TOKENS, S_HEADS, POOL, HD).mean(axis=2).reshape(TOKENS, S_HEADS * HD)
    weight = (weight_codes.astype(jnp.float32) * jnp.exp2(-scale_exponents.astype(jnp.float32))[None, :] / math.sqrt(D_S)).astype(jnp.bfloat16)
    clipped = jnp.clip(student_hidden, -4.0, 4.0)
    projected = jnp.dot(clipped, weight, preferred_element_type=jnp.float32)
    student_out = projected.astype(jnp.bfloat16)
    residue = (projected - target).astype(jnp.bfloat16)
    weight_grad = jnp.dot(clipped.T, residue, preferred_element_type=jnp.float32) / math.sqrt(TOKENS)
    return (teacher_context, student_out, weight_grad)
```

```python
import math

import jax
import jax.numpy as jnp
from jax import lax
from jax.experimental import pallas as pl
from jax.experimental.pallas import tpu as pltpu
from jax.sharding import Mesh
from jax.sharding import PartitionSpec as P

HEADS = 64
KV_HEADS = 8
GROUP = HEADS // KV_HEADS
HD = 128
D_S = 4096
POOL = 4
TOK = 128
NY, NZ, NC, NW, NX = 4, 8, 2, 2, 4
CLIP = 4.0
SCALE_LOG2 = math.log2(math.e) / math.sqrt(HD)
LOWEST = -1e30

CTX = ("y", "z", "c")
HEAD = ("w", "x")


def attend_kernel(place_ref, q_ref, kv0_ref, kv1_ref, out_ref, target_ref, top_ref, acc_ref):
    y, z, c = place_ref[0], place_ref[1], place_ref[2]

    def head_step(head, key, value, mask, first):
        query = q_ref[:, head * HD : (head + 1) * HD]
        scores = lax.dot_general(
            query, key, (((1,), (1,)), ((), ())), preferred_element_type=jnp.float32
        )
        if mask is not None:
            scores = jnp.where(mask, scores, LOWEST)
        block_top = jnp.max(scores, axis=1, keepdims=True)
        if first:
            top = block_top
        else:
            top_old = top_ref[head][:, :1]
            top = jnp.maximum(top_old, block_top)
        prob = jnp.exp2(scores * SCALE_LOG2 - top * SCALE_LOG2).astype(jnp.bfloat16)
        part = jnp.dot(prob, value, preferred_element_type=jnp.float32)
        if first:
            acc_ref[head] = part
        else:
            shrink = jnp.exp2((top_old - top) * SCALE_LOG2)
            acc_ref[head] = acc_ref[head] * shrink + part
        top_ref[head] = jnp.broadcast_to(top, (TOK, HD))

    def blocks(slab, first_row, rows):
        key = jnp.concatenate(
            [ref[slab, 0, pl.ds(first_row, rows)].reshape(rows * TOK, HD) for ref in (kv0_ref, kv1_ref)]
        )
        value = jnp.concatenate(
            [ref[slab, 1, pl.ds(first_row, rows)].reshape(rows * TOK, HD) for ref in (kv0_ref, kv1_ref)]
        )
        ones = jnp.ones((2 * rows * TOK, HD), jnp.bfloat16)
        return key, jnp.concatenate([value, ones], axis=1)

    key, value = blocks(z, y, 1)
    key_pos = lax.broadcasted_iota(jnp.int32, (TOK, 2 * TOK), 1)
    query_pos = lax.broadcasted_iota(jnp.int32, (TOK, 2 * TOK), 0) + c * TOK
    mask = key_pos <= query_pos
    for head in range(GROUP):
        head_step(head, key, value, mask, True)

    def slab_step(slab, _):
        rows_here = y + (slab < z).astype(jnp.int32)
        for rows in range(1, NY + 1):

            @pl.when(rows_here == rows)
            def _():
                key, value = blocks(slab, 0, rows)
                for head in range(GROUP):
                    head_step(head, key, value, None, False)

        return 0

    lax.fori_loop(0, NZ, slab_step, 0)
    for pool in range(GROUP // POOL):
        mean = jnp.zeros((TOK, HD), jnp.float32)
        for head in range(pool * POOL, (pool + 1) * POOL):
            context = (acc_ref[head, :, :HD] / acc_ref[head, :, HD:]).astype(jnp.bfloat16)
            out_ref[:, head * HD : (head + 1) * HD] = context
            mean = mean + context.astype(jnp.float32)
        target_ref[:, pool * HD : (pool + 1) * HD] = mean * (1.0 / POOL)


def attend(place, query, kv0, kv1):
    vmem = pl.BlockSpec(memory_space=pltpu.VMEM)
    return pl.pallas_call(
        attend_kernel,
        out_shape=(
            jax.ShapeDtypeStruct((TOK, GROUP * HD), jnp.bfloat16),
            jax.ShapeDtypeStruct((TOK, GROUP // POOL * HD), jnp.float32),
        ),
        in_specs=[pl.BlockSpec(memory_space=pltpu.SMEM), vmem, vmem, vmem],
        out_specs=(vmem, vmem),
        scratch_shapes=[
            pltpu.VMEM((GROUP, TOK, HD), jnp.float32),
            pltpu.VMEM((GROUP, TOK, 2 * HD), jnp.float32),
        ],
        compiler_params=pltpu.CompilerParams(vmem_limit_bytes=40 * 1024 * 1024),
        cost_estimate=pl.CostEstimate(
            flops=4 * GROUP * TOK * 8192 * HD, bytes_accessed=5 << 20, transcendentals=GROUP * TOK * 8192
        ),
    )(place, query, kv0, kv1)


def shift(array, axis, size, step):
    return lax.ppermute(array, axis, [(i, (i + step) % size) for i in range(size)])


def per_device(query, key, value, hidden, codes, exponents):
    y, z, c = lax.axis_index("y"), lax.axis_index("z"), lax.axis_index("c")
    w, x = lax.axis_index("w"), lax.axis_index("x")

    own = jnp.stack([key, value])
    lower = [
        lax.ppermute(own, "y", [(i, i + step) for i in range(NY - step)]) for step in range(1, NY)
    ]
    by_step = jnp.stack([own] + lower)
    rows = jnp.stack(
        [lax.dynamic_index_in_dim(by_step, jnp.maximum(y - row, 0), 0, keepdims=False) for row in range(NY)],
        axis=1,
    )
    slabs = lax.all_gather(rows, "z", axis=0, tiled=False)
    other = shift(slabs, "c", NC, 1)
    kv0 = jnp.where(c == 0, slabs, other)
    kv1 = jnp.where(c == 0, other, slabs)
    teacher_context, target = attend(jnp.stack([y, z, c]), query, kv0, kv1)

    clipped = jnp.clip(hidden, -CLIP, CLIP)
    chunks = (
        clipped.reshape(16, NY, NZ, NC, 64).transpose(1, 3, 0, 2, 4).reshape(NY * NC, 16, NZ * 64)
    )
    chunks = lax.all_to_all(chunks, ("y", "c"), 0, 0)
    pair = jnp.stack([chunks, shift(chunks, "w", NW, 1)])
    around = jnp.stack([pair] + [shift(pair, "x", NX, step) for step in range(1, NX)])
    around = around.reshape(NX * NW, NY * NC, 16, NZ * 64)
    part = [
        lax.dynamic_index_in_dim(around, (x - xx) % NX * NW + (w - ww) % NW, 0, keepdims=False)
        for ww in range(NW)
        for xx in range(NX)
    ]
    columns = jnp.stack(part, axis=1).reshape(NY * NC * TOK, NZ * 64)

    weight = (
        codes.astype(jnp.float32) * jnp.exp2(-exponents.astype(jnp.float32))[None, :] / math.sqrt(D_S)
    ).astype(jnp.bfloat16)
    weight = lax.all_gather(weight, "z", axis=0, tiled=True)
    partial = jnp.dot(columns, weight, preferred_element_type=jnp.float32)
    partial = partial.astype(jnp.bfloat16).reshape(NY * NC, TOK, -1)
    projected = jnp.sum(lax.all_to_all(partial, ("y", "c"), 0, 0).astype(jnp.float32), axis=0)
    student_out = lax.all_to_all(
        projected.astype(jnp.bfloat16), HEAD, split_axis=0, concat_axis=1, tiled=True
    )

    residue = (projected - target).astype(jnp.bfloat16)
    residue = lax.all_gather(residue, ("y", "c"), axis=0, tiled=True)
    grad = lax.dot_general(
        columns, residue, (((0,), (0,)), ((), ())), preferred_element_type=jnp.float32
    ) * (1.0 / math.sqrt(NY * NZ * NC * TOK))
    grad = grad.astype(jnp.bfloat16).reshape(NZ, 64, -1)
    weight_grad = jnp.sum(lax.all_to_all(grad, "z", 0, 0).astype(jnp.float32), axis=0)
    return teacher_context, student_out, weight_grad


def solution(mesh):
    fine = Mesh(mesh.devices.reshape(NY, NZ, NC, NW, NX), ("y", "z", "c", "w", "x"))
    return jax.shard_map(
        per_device,
        mesh=fine,
        in_specs=(
            P(CTX, HEAD),
            P(CTX, HEAD),
            P(CTX, HEAD),
            P(CTX + HEAD, None),
            P(CTX, HEAD),
            P(HEAD),
        ),
        out_specs=(P(CTX, HEAD), P(CTX + HEAD, None), P(CTX, HEAD)),
        check_vma=False,
    )
```

```python
import functools
import math

import jax
import jax.numpy as jnp
from jax import lax
from jax.experimental import pallas as pl
from jax.experimental.pallas import tpu as pltpu
from jax.sharding import Mesh
from jax.sharding import PartitionSpec as P

HEADS = 64
KV_HEADS = 8
GROUP = HEADS // KV_HEADS
HD = 128
D_S = 4096
POOL = 4
TOK = 128
FEAT = 64
SHARE = 16
NY, NZ, NC, NW, NX = 4, 8, 2, 2, 4
CLIP = 4.0
SCALE_LOG2 = math.log2(math.e) / math.sqrt(HD)
LOWEST = -1e30

CTX = ("y", "z", "c")
HEAD = ("w", "x")


def attend_kernel(plan, first_call, last_call, place_ref, q_ref, *refs):
    y, z, c = place_ref[0], place_ref[1], place_ref[2]
    slabs, refs = refs[: sum(parts for _, parts in plan)], refs[sum(parts for _, parts in plan) :]
    if not first_call:
        (top_in, acc_in), refs = refs[:2], refs[2:]
    if last_call:
        out_ref, target_ref, top_ref, acc_ref = refs
    else:
        top_ref, acc_ref = refs
    if not first_call:
        top_ref[...] = top_in[...]
        acc_ref[...] = acc_in[...]

    def all_heads(key, value, mask):
        count = key.shape[0] // HD
        value = jnp.concatenate([value, jnp.ones_like(value)], axis=1)
        for head in range(GROUP):
            query = q_ref[:, head * HD : (head + 1) * HD]
            scores = lax.dot_general(
                query, key, (((1,), (1,)), ((), ())), preferred_element_type=jnp.float32
            )
            if mask is not None:
                scores = jnp.where(mask, scores, LOWEST)
            tiles = [scores[:, i * HD : (i + 1) * HD] for i in range(count)]
            top = tiles[0]
            for tile in tiles[1:]:
                top = jnp.maximum(top, tile)
            top = jnp.broadcast_to(jnp.max(top, axis=1, keepdims=True), (TOK, HD))
            if mask is None:
                top_old = top_ref[head]
                top = jnp.maximum(top, top_old)
            scaled = top * SCALE_LOG2
            prob = jnp.concatenate(
                [jnp.exp2(tile * SCALE_LOG2 - scaled).astype(jnp.bfloat16) for tile in tiles], axis=1
            )
            part = jnp.dot(prob, value, preferred_element_type=jnp.float32)
            if mask is None:
                shrink = jnp.exp2(top_old * SCALE_LOG2 - scaled)
                acc_ref[head] = acc_ref[head] * jnp.concatenate([shrink, shrink], axis=1) + part
            else:
                acc_ref[head] = part
            top_ref[head] = top

    def blocks(parts, row, rows):
        return [
            jnp.concatenate([part[pl.ds(row, rows), which].reshape(rows * TOK, HD) for part in parts])
            for which in (0, 1)
        ]

    at = 0
    for steps, count in plan:
        refs_here = slabs[at : at + count]
        at += count
        parts = refs_here if count == NC else [refs_here[0].at[core] for core in range(NC)]
        if steps == 0:
            key_pos = lax.broadcasted_iota(jnp.int32, (TOK, NC * TOK), 1)
            query_pos = lax.broadcasted_iota(jnp.int32, (TOK, NC * TOK), 0) + c * TOK
            all_heads(*blocks(parts, 0, 1), key_pos <= query_pos)
            first_row = jnp.int32(1)
        else:
            source = (z + steps * (2 * c - 1) + NZ) % NZ
            first_row = (source > z).astype(jnp.int32)
        rows = y + 1 - first_row

        def two_rows(i, _, parts=parts, first_row=first_row):
            all_heads(*blocks(parts, first_row + 2 * i, 2), None)
            return 0

        lax.fori_loop(0, rows // 2, two_rows, 0)

        @pl.when(rows % 2 == 1)
        def _(parts=parts):
            all_heads(*blocks(parts, y, 1), None)

    if last_call:
        for pool in range(GROUP // POOL):
            mean = jnp.zeros((TOK, HD), jnp.float32)
            for head in range(pool * POOL, (pool + 1) * POOL):
                context = (acc_ref[head, :, :HD] / acc_ref[head, :, HD:]).astype(jnp.bfloat16)
                out_ref[:, head * HD : (head + 1) * HD] = context
                mean = mean + context.astype(jnp.float32)
            target_ref[:, pool * HD : (pool + 1) * HD] = mean * (1.0 / POOL)


def attend(place, query, plan, slabs, state, last_call=False):
    vmem = pl.BlockSpec(memory_space=pltpu.VMEM)
    state_shape = (
        jax.ShapeDtypeStruct((GROUP, TOK, HD), jnp.float32),
        jax.ShapeDtypeStruct((GROUP, TOK, 2 * HD), jnp.float32),
    )
    result_shape = (
        jax.ShapeDtypeStruct((TOK, GROUP * HD), jnp.bfloat16),
        jax.ShapeDtypeStruct((TOK, GROUP // POOL * HD), jnp.float32),
    )
    state = () if state is None else tuple(state)
    return pl.pallas_call(
        functools.partial(attend_kernel, plan, not state, last_call),
        out_shape=result_shape if last_call else state_shape,
        in_specs=[pl.BlockSpec(memory_space=pltpu.SMEM)] + [vmem] * (1 + len(slabs) + len(state)),
        out_specs=(vmem, vmem),
        scratch_shapes=[pltpu.VMEM(leaf.shape, leaf.dtype) for leaf in state_shape] if last_call else [],
        compiler_params=pltpu.CompilerParams(vmem_limit_bytes=24 * 1024 * 1024),
        cost_estimate=pl.CostEstimate(
            flops=len(plan) * 8 * GROUP * TOK * 1024 * HD,
            bytes_accessed=4 << 20,
            transcendentals=len(plan) * GROUP * TOK * 1024,
        ),
    )(place, query, *slabs, *state)


def project_kernel(place_ref, *refs):
    pieces, (weight_ref, columns_ref, partial_ref) = refs[:NX], refs[NX:]
    y, x = place_ref[0], place_ref[4]
    for step in range(NX):
        columns_ref[:, :, pl.ds((x + NX - step) % NX, 1)] = pieces[step][...][:, :, None]
    weight = []
    for row in range(NY):
        for core in range(NC):
            block = weight_ref[core, (y + NY - row) % NY]
            weight.append(jnp.concatenate([block[:FEAT], block[FEAT:]], axis=1))
    weight = jnp.concatenate(weight)
    for slab in range(NZ):
        rows = columns_ref[slab].reshape(TOK, NY * NC * FEAT)
        partial_ref[slab] = jnp.dot(rows, weight, preferred_element_type=jnp.float32).astype(jnp.bfloat16)


def project(place, pieces, weight):
    vmem = pl.BlockSpec(memory_space=pltpu.VMEM)
    return pl.pallas_call(
        project_kernel,
        out_shape=(
            jax.ShapeDtypeStruct((NZ, NW, NX, SHARE, NY * NC * FEAT), jnp.bfloat16),
            jax.ShapeDtypeStruct((NZ, TOK, 2 * HD), jnp.bfloat16),
        ),
        in_specs=[pl.BlockSpec(memory_space=pltpu.SMEM)] + [vmem] * (NX + 1),
        out_specs=(vmem, vmem),
        compiler_params=pltpu.CompilerParams(vmem_limit_bytes=24 * 1024 * 1024),
        cost_estimate=pl.CostEstimate(
            flops=2 * NZ * TOK * 512 * 256, bytes_accessed=3 << 20, transcendentals=0
        ),
    )(place, *pieces, weight)


def shift(array, axis, size, step):
    return lax.ppermute(array, axis, [(i, (i + step) % size) for i in range(size)])


def round_z(array):
    pairs = [(i * NC, (i + 1) % NZ * NC) for i in range(NZ)]
    pairs += [(i * NC + 1, (i - 1) % NZ * NC + 1) for i in range(NZ)]
    return lax.ppermute(array, ("z", "c"), pairs)


def per_device(query, key, value, hidden, codes, exponents):
    y, z, c = lax.axis_index("y"), lax.axis_index("z"), lax.axis_index("c")
    w, x = lax.axis_index("w"), lax.axis_index("x")
    place = jnp.stack([y, z, c, w, x])
    after = lax.optimization_barrier

    weight = (
        codes.astype(jnp.float32) * jnp.exp2(-exponents.astype(jnp.float32))[None, :] / math.sqrt(D_S)
    ).astype(jnp.bfloat16)
    weight = jnp.concatenate([weight[:, :HD], weight[:, HD:]])
    own = jnp.stack([key, value, weight])
    rows = jnp.stack([own] + [shift(own, "y", NY, step) for step in range(1, NY)])
    both = lax.all_gather(rows, "c", axis=0, tiled=False)
    slab, weight_rows = both[:, :, :2], both[:, :, 2]

    clipped = jnp.clip(hidden, -CLIP, CLIP)
    chunks = (
        clipped.reshape(SHARE, NY, NZ, NC, FEAT).transpose(2, 0, 1, 3, 4).reshape(NZ, SHARE, NY * NC * FEAT)
    )
    swapped = shift(chunks, "w", NW, 1)
    pair = jnp.stack(
        [jnp.where(w == 0, chunks, swapped), jnp.where(w == 0, swapped, chunks)], axis=1
    )

    slab, pair = after((slab, pair))
    near = round_z(slab)
    pair = lax.all_to_all(pair, "z", 0, 0)
    near, pair = after((near, pair))
    far = round_z(near)
    near_other = shift(near, "c", NC, 1)
    pieces = [pair] + [shift(pair, "x", NX, step) for step in range(1, NX)]
    state = attend(place, query, ((0, 1), (1, 1)), (slab, near), None)

    state, far, *pieces = after((state, far, *pieces))
    columns, partial = project(place, pieces, weight_rows)
    columns = columns.reshape(NZ * TOK, NY * NC * FEAT)
    partial, state, far = after((partial, state, far))
    received = lax.all_to_all(partial, "z", 0, 0)
    third = round_z(far)
    far_other = shift(far, "c", NC, 1)
    state = attend(place, query, ((-1, 1), (2, 1)), (near_other, far), state)

    state, third = after((state, third))
    fourth = round_z(jnp.where(c == 0, third[0], third[1]))
    third_other = shift(third, "c", NC, 1)
    state = attend(place, query, ((-2, 1), (3, 1)), (far_other, third), state)

    state, fourth, received = after((state, fourth, received))
    fourth_other = shift(fourth, "c", NC, 1)
    projected = jnp.sum(received.astype(jnp.float32), axis=0)
    student = lax.all_to_all(
        projected.astype(jnp.bfloat16).reshape(NW * NX, SHARE, -1), HEAD, 0, 0
    )
    teacher_context, target = attend(
        place, query, ((-3, 1), (4, 2)), (third_other, fourth, fourth_other), state, last_call=True
    )

    target, student = after((target, student))
    student_out = student.transpose(1, 0, 2).reshape(SHARE, -1)
    residue = (projected - target).astype(jnp.bfloat16)
    residue = lax.all_to_all(jnp.broadcast_to(residue[None], (NZ,) + residue.shape), "z", 0, 0)
    grad = lax.dot_general(
        columns,
        residue.reshape(NZ * TOK, -1),
        (((0,), (0,)), ((), ())),
        preferred_element_type=jnp.float32,
    ) * (1.0 / math.sqrt(NY * NZ * NC * TOK))
    grad = grad.astype(jnp.bfloat16).reshape(NY * NC, FEAT, -1)
    weight_grad = jnp.sum(lax.all_to_all(grad, ("y", "c"), 0, 0).astype(jnp.float32), axis=0)
    return teacher_context, student_out, weight_grad


def solution(mesh):
    fine = Mesh(mesh.devices.reshape(NY, NZ, NC, NW, NX), ("y", "z", "c", "w", "x"))
    return jax.shard_map(
        per_device,
        mesh=fine,
        in_specs=(
            P(CTX, HEAD),
            P(CTX, HEAD),
            P(CTX, HEAD),
            P(CTX + HEAD, None),
            P(CTX, HEAD),
            P(HEAD),
        ),
        out_specs=(P(CTX, HEAD), P(CTX + HEAD, None), P(CTX, HEAD)),
        check_vma=False,
    )
```

```python
import functools
import math

import jax
import jax.numpy as jnp
from jax import lax
from jax.experimental import pallas as pl
from jax.experimental.pallas import tpu as pltpu
from jax.sharding import Mesh
from jax.sharding import PartitionSpec as P

HEADS = 64
KV_HEADS = 8
GROUP = HEADS // KV_HEADS
HD = 128
D_S = 4096
POOL = 4
TOK = 128
FEAT = 64
SHARE = 16
NY, NZ, NC, NW, NX = 4, 8, 2, 2, 4
CLIP = 4.0
SCALE_LOG2 = math.log2(math.e) / math.sqrt(HD)
LOWEST = -1e30

CTX = ("y", "z", "c")
HEAD = ("w", "x")


def attend_kernel(plan, first_call, last_call, place_ref, q_ref, *refs):
    y, z, c = place_ref[0], place_ref[1], place_ref[2]
    count = 1 + max(ref for _, parts in plan for ref, _ in parts)
    slabs, refs = refs[:count], refs[count:]
    if not first_call:
        (top_in, acc_in), refs = refs[:2], refs[2:]
    if last_call:
        out_ref, target_ref, top_ref, acc_ref = refs
    else:
        top_ref, acc_ref = refs
    if not first_call:
        top_ref[...] = top_in[...]
        acc_ref[...] = acc_in[...]

    def all_heads(key, value, mask):
        count = key.shape[0] // HD
        value = jnp.concatenate([value, jnp.ones_like(value)], axis=1)
        for head in range(GROUP):
            query = q_ref[:, head * HD : (head + 1) * HD]
            scores = lax.dot_general(
                query, key, (((1,), (1,)), ((), ())), preferred_element_type=jnp.float32
            )
            if mask is not None:
                scores = jnp.where(mask, scores, LOWEST)
            tiles = [scores[:, i * HD : (i + 1) * HD] for i in range(count)]
            top = tiles[0]
            for tile in tiles[1:]:
                top = jnp.maximum(top, tile)
            top = jnp.broadcast_to(jnp.max(top, axis=1, keepdims=True), (TOK, HD))
            if mask is None:
                top_old = top_ref[head]
                top = jnp.maximum(top, top_old)
            scaled = top * SCALE_LOG2
            prob = jnp.concatenate(
                [jnp.exp2(tile * SCALE_LOG2 - scaled).astype(jnp.bfloat16) for tile in tiles], axis=1
            )
            part = jnp.dot(prob, value, preferred_element_type=jnp.float32)
            if mask is None:
                shrink = jnp.exp2(top_old * SCALE_LOG2 - scaled)
                acc_ref[head] = acc_ref[head] * jnp.concatenate([shrink, shrink], axis=1) + part
            else:
                acc_ref[head] = part
            top_ref[head] = top

    def blocks(parts, row, rows):
        return [
            jnp.concatenate([part[pl.ds(row, rows), which].reshape(rows * TOK, HD) for part in parts])
            for which in (0, 1)
        ]

    for steps, parts in plan:
        parts = [slabs[ref].at[path] if path else slabs[ref] for ref, path in parts]
        if steps == 0:
            key_pos = lax.broadcasted_iota(jnp.int32, (TOK, NC * TOK), 1)
            query_pos = lax.broadcasted_iota(jnp.int32, (TOK, NC * TOK), 0) + c * TOK
            all_heads(*blocks(parts, 0, 1), key_pos <= query_pos)
            first_row = jnp.int32(1)
        else:
            source = (z + steps * (2 * c - 1) + NZ) % NZ
            first_row = (source > z).astype(jnp.int32)
        rows = y + 1 - first_row

        def two_rows(i, _, parts=parts, first_row=first_row):
            all_heads(*blocks(parts, first_row + 2 * i, 2), None)
            return 0

        lax.fori_loop(0, rows // 2, two_rows, 0)

        @pl.when(rows % 2 == 1)
        def _(parts=parts):
            all_heads(*blocks(parts, y, 1), None)

    if last_call:
        for pool in range(GROUP // POOL):
            mean = jnp.zeros((TOK, HD), jnp.float32)
            for head in range(pool * POOL, (pool + 1) * POOL):
                context = (acc_ref[head, :, :HD] / acc_ref[head, :, HD:]).astype(jnp.bfloat16)
                out_ref[:, head * HD : (head + 1) * HD] = context
                mean = mean + context.astype(jnp.float32)
            target_ref[:, pool * HD : (pool + 1) * HD] = mean * (1.0 / POOL)


def attend(place, query, plan, slabs, state, last_call=False):
    vmem = pl.BlockSpec(memory_space=pltpu.VMEM)
    state_shape = (
        jax.ShapeDtypeStruct((GROUP, TOK, HD), jnp.float32),
        jax.ShapeDtypeStruct((GROUP, TOK, 2 * HD), jnp.float32),
    )
    result_shape = (
        jax.ShapeDtypeStruct((TOK, GROUP * HD), jnp.bfloat16),
        jax.ShapeDtypeStruct((TOK, GROUP // POOL * HD), jnp.float32),
    )
    state = () if state is None else tuple(state)
    return pl.pallas_call(
        functools.partial(attend_kernel, plan, not state, last_call),
        out_shape=result_shape if last_call else state_shape,
        in_specs=[pl.BlockSpec(memory_space=pltpu.SMEM)] + [vmem] * (1 + len(slabs) + len(state)),
        out_specs=(vmem, vmem),
        scratch_shapes=[pltpu.VMEM(leaf.shape, leaf.dtype) for leaf in state_shape] if last_call else [],
        compiler_params=pltpu.CompilerParams(vmem_limit_bytes=24 * 1024 * 1024),
        cost_estimate=pl.CostEstimate(
            flops=len(plan) * 8 * GROUP * TOK * 1024 * HD,
            bytes_accessed=4 << 20,
            transcendentals=len(plan) * GROUP * TOK * 1024,
        ),
    )(place, query, *slabs, *state)


def project_kernel(place_ref, *refs):
    pieces, (weight_ref, columns_ref, partial_ref) = refs[:NX], refs[NX:]
    y, x = place_ref[0], place_ref[4]
    for step in range(NX):
        columns_ref[:, :, pl.ds((x + NX - step) % NX, 1)] = pieces[step][...][:, :, None]
    weight = []
    for row in range(NY):
        for core in range(NC):
            block = weight_ref[core, (y + NY - row) % NY]
            weight.append(jnp.concatenate([block[:FEAT], block[FEAT:]], axis=1))
    weight = jnp.concatenate(weight)
    for slab in range(NZ):
        rows = columns_ref[slab].reshape(TOK, NY * NC * FEAT)
        partial_ref[slab] = jnp.dot(rows, weight, preferred_element_type=jnp.float32).astype(jnp.bfloat16)


def project(place, pieces, weight):
    vmem = pl.BlockSpec(memory_space=pltpu.VMEM)
    return pl.pallas_call(
        project_kernel,
        out_shape=(
            jax.ShapeDtypeStruct((NZ, NW, NX, SHARE, NY * NC * FEAT), jnp.bfloat16),
            jax.ShapeDtypeStruct((NZ, TOK, 2 * HD), jnp.bfloat16),
        ),
        in_specs=[pl.BlockSpec(memory_space=pltpu.SMEM)] + [vmem] * (NX + 1),
        out_specs=(vmem, vmem),
        compiler_params=pltpu.CompilerParams(vmem_limit_bytes=24 * 1024 * 1024),
        cost_estimate=pl.CostEstimate(
            flops=2 * NZ * TOK * 512 * 256, bytes_accessed=3 << 20, transcendentals=0
        ),
    )(place, *pieces, weight)


def pack_kernel(key_ref, value_ref, codes_ref, exponents_ref, own_ref):
    own_ref[0] = key_ref[...]
    own_ref[1] = value_ref[...]
    scale = jnp.exp2(-exponents_ref[...].astype(jnp.float32)) / math.sqrt(D_S)
    weight = (codes_ref[...].astype(jnp.float32) * scale).astype(jnp.bfloat16)
    own_ref[2, :FEAT] = weight[:, :HD]
    own_ref[2, FEAT:] = weight[:, HD:]


def pack(key, value, codes, exponents):
    vmem = pl.BlockSpec(memory_space=pltpu.VMEM)
    return pl.pallas_call(
        pack_kernel,
        out_shape=jax.ShapeDtypeStruct((3, TOK, HD), jnp.bfloat16),
        in_specs=[vmem] * 4,
        out_specs=vmem,
    )(key, value, codes, exponents.reshape(1, -1))


def shift(array, axis, size, step):
    return lax.ppermute(array, axis, [(i, (i + step) % size) for i in range(size)])


def round_z(array):
    pairs = [(i * NC, (i + 1) % NZ * NC) for i in range(NZ)]
    pairs += [(i * NC + 1, (i - 1) % NZ * NC + 1) for i in range(NZ)]
    return lax.ppermute(array, ("z", "c"), pairs)


def per_device(query, key, value, hidden, codes, exponents):
    y, z, c = lax.axis_index("y"), lax.axis_index("z"), lax.axis_index("c")
    w, x = lax.axis_index("w"), lax.axis_index("x")
    place = jnp.stack([y, z, c, w, x])
    after = lax.optimization_barrier

    own = pack(key, value, codes, exponents)
    rows = jnp.stack([own] + [shift(own, "y", NY, step) for step in range(1, NY)])
    both = lax.all_gather(rows, "c", axis=0, tiled=False)
    slab, weight_rows = both[:, :, :2], both[:, :, 2]

    clipped = jnp.clip(hidden, -CLIP, CLIP)
    chunks = (
        clipped.reshape(SHARE, NY, NZ, NC, FEAT).transpose(2, 0, 1, 3, 4).reshape(NZ, SHARE, NY * NC * FEAT)
    )
    swapped = shift(chunks, "w", NW, 1)
    pair = jnp.stack(
        [jnp.where(w == 0, chunks, swapped), jnp.where(w == 0, swapped, chunks)], axis=1
    )

    def slab_in(ref, *path):
        return tuple((ref, path + (core,)) for core in range(NC))

    slab, pair = after((slab, pair))
    near = round_z(slab)
    pair = lax.all_to_all(pair, "z", 0, 0)
    near, pair = after((near, pair))
    far = round_z(near)
    pieces = [pair] + [shift(pair, "x", NX, step) for step in range(1, NX)]
    state = attend(place, query, ((0, slab_in(0)), (1, slab_in(1))), (slab, near), None)

    state, far, *pieces = after((state, far, *pieces))
    columns, partial = project(place, pieces, weight_rows)
    columns = columns.reshape(NZ * TOK, NY * NC * FEAT)
    partial, state, far = after((partial, state, far))
    received = lax.all_to_all(partial, "z", 0, 0)
    third = round_z(far)
    two_other = shift(jnp.stack([near, far]), "c", NC, 1)
    state = attend(place, query, ((2, slab_in(0)),), (far,), state)

    state, third = after((state, third))
    fourth = round_z(jnp.where(c == 0, third[0], third[1]))
    state = attend(
        place, query, ((3, slab_in(0)), (-1, slab_in(1, 0)), (-2, slab_in(1, 1))), (third, two_other), state
    )

    state, third, fourth, received = after((state, third, fourth, received))
    last_other = shift(jnp.concatenate([third, fourth[None]]), "c", NC, 1)
    projected = jnp.sum(received.astype(jnp.float32), axis=0)
    student = lax.all_to_all(
        projected.astype(jnp.bfloat16).reshape(NW * NX, SHARE, -1), HEAD, 0, 0
    )
    teacher_context, target = attend(
        place,
        query,
        ((-3, slab_in(1)), (4, ((0, ()), (1, (NC,))))),
        (fourth, last_other),
        state,
        last_call=True,
    )

    target, student = after((target, student))
    student_out = student.transpose(1, 0, 2).reshape(SHARE, -1)
    residue = (projected - target).astype(jnp.bfloat16)
    residue = lax.all_to_all(jnp.broadcast_to(residue[None], (NZ,) + residue.shape), "z", 0, 0)
    grad = lax.dot_general(
        columns,
        residue.reshape(NZ * TOK, -1),
        (((0,), (0,)), ((), ())),
        preferred_element_type=jnp.float32,
    ) * (1.0 / math.sqrt(NY * NZ * NC * TOK))
    grad = grad.astype(jnp.bfloat16).reshape(NY * NC, FEAT, -1)
    weight_grad = jnp.sum(lax.all_to_all(grad, ("y", "c"), 0, 0).astype(jnp.float32), axis=0)
    return teacher_context, student_out, weight_grad


def solution(mesh):
    fine = Mesh(mesh.devices.reshape(NY, NZ, NC, NW, NX), ("y", "z", "c", "w", "x"))
    return jax.shard_map(
        per_device,
        mesh=fine,
        in_specs=(
            P(CTX, HEAD),
            P(CTX, HEAD),
            P(CTX, HEAD),
            P(CTX + HEAD, None),
            P(CTX, HEAD),
            P(HEAD),
        ),
        out_specs=(P(CTX, HEAD), P(CTX + HEAD, None), P(CTX, HEAD)),
        check_vma=False,
    )
```

```python
import functools
import math

import jax
import jax.numpy as jnp
from jax import lax
from jax.experimental import pallas as pl
from jax.experimental.pallas import tpu as pltpu
from jax.sharding import Mesh
from jax.sharding import PartitionSpec as P

HEADS = 64
KV_HEADS = 8
GROUP = HEADS // KV_HEADS
HD = 128
D_S = 4096
POOL = 4
TOK = 128
FEAT = 64
SHARE = 16
NY, NZ, NC, NW, NX = 4, 8, 2, 2, 4
CLIP = 4.0
SCALE_LOG2 = math.log2(math.e) / math.sqrt(HD)
LOWEST = -1e30

CTX = ("y", "z", "c")
HEAD = ("w", "x")


def attend_kernel(plan, first_call, last_call, place_ref, q_ref, *refs):
    y, z, c = place_ref[0], place_ref[1], place_ref[2]
    count = 1 + max(ref for _, parts in plan for ref, _ in parts)
    slabs, refs = refs[:count], refs[count:]
    if not first_call:
        (top_in, acc_in), refs = refs[:2], refs[2:]
    if last_call:
        out_ref, target_ref, top_ref, acc_ref = refs
    else:
        top_ref, acc_ref = refs
    if not first_call:
        top_ref[...] = top_in[...]
        acc_ref[...] = acc_in[...]

    def all_heads(key, value, mask):
        count = key.shape[0] // HD
        value = jnp.concatenate([value, jnp.ones_like(value)], axis=1)
        for head in range(GROUP):
            query = q_ref[:, head * HD : (head + 1) * HD]
            scores = lax.dot_general(
                query, key, (((1,), (1,)), ((), ())), preferred_element_type=jnp.float32
            )
            if mask is not None:
                scores = jnp.where(mask, scores, LOWEST)
            tiles = [scores[:, i * HD : (i + 1) * HD] for i in range(count)]
            top = tiles[0]
            for tile in tiles[1:]:
                top = jnp.maximum(top, tile)
            top = jnp.broadcast_to(jnp.max(top, axis=1, keepdims=True), (TOK, HD))
            if mask is None:
                top_old = top_ref[head]
                top = jnp.maximum(top, top_old)
            scaled = top * SCALE_LOG2
            prob = jnp.concatenate(
                [jnp.exp2(tile * SCALE_LOG2 - scaled).astype(jnp.bfloat16) for tile in tiles], axis=1
            )
            part = jnp.dot(prob, value, preferred_element_type=jnp.float32)
            if mask is None:
                shrink = jnp.exp2(top_old * SCALE_LOG2 - scaled)
                acc_ref[head] = acc_ref[head] * jnp.concatenate([shrink, shrink], axis=1) + part
            else:
                acc_ref[head] = part
            top_ref[head] = top

    def blocks(parts, row, rows):
        return [
            jnp.concatenate([part[pl.ds(row, rows), which].reshape(rows * TOK, HD) for part in parts])
            for which in (0, 1)
        ]

    for steps, parts in plan:
        parts = [slabs[ref].at[path] if path else slabs[ref] for ref, path in parts]
        if steps == 0:
            key_pos = lax.broadcasted_iota(jnp.int32, (TOK, NC * TOK), 1)
            query_pos = lax.broadcasted_iota(jnp.int32, (TOK, NC * TOK), 0) + c * TOK
            all_heads(*blocks(parts, 0, 1), key_pos <= query_pos)
            first_row = jnp.int32(1)
        else:
            source = (z + steps * (2 * c - 1) + NZ) % NZ
            first_row = (source > z).astype(jnp.int32)
        rows = y + 1 - first_row

        def two_rows(i, _, parts=parts, first_row=first_row):
            all_heads(*blocks(parts, first_row + 2 * i, 2), None)
            return 0

        lax.fori_loop(0, rows // 2, two_rows, 0)

        @pl.when(rows % 2 == 1)
        def _(parts=parts):
            all_heads(*blocks(parts, y, 1), None)

    if last_call:
        for pool in range(GROUP // POOL):
            mean = jnp.zeros((TOK, HD), jnp.float32)
            for head in range(pool * POOL, (pool + 1) * POOL):
                context = (acc_ref[head, :, :HD] / acc_ref[head, :, HD:]).astype(jnp.bfloat16)
                out_ref[:, head * HD : (head + 1) * HD] = context
                mean = mean + context.astype(jnp.float32)
            target_ref[:, pool * HD : (pool + 1) * HD] = mean * (1.0 / POOL)


def attend(place, query, plan, slabs, state, last_call=False):
    vmem = pl.BlockSpec(memory_space=pltpu.VMEM)
    state_shape = (
        jax.ShapeDtypeStruct((GROUP, TOK, HD), jnp.float32),
        jax.ShapeDtypeStruct((GROUP, TOK, 2 * HD), jnp.float32),
    )
    result_shape = (
        jax.ShapeDtypeStruct((TOK, GROUP * HD), jnp.bfloat16),
        jax.ShapeDtypeStruct((TOK, GROUP // POOL * HD), jnp.float32),
    )
    state = () if state is None else tuple(state)
    return pl.pallas_call(
        functools.partial(attend_kernel, plan, not state, last_call),
        out_shape=result_shape if last_call else state_shape,
        in_specs=[pl.BlockSpec(memory_space=pltpu.SMEM)] + [vmem] * (1 + len(slabs) + len(state)),
        out_specs=(vmem, vmem),
        scratch_shapes=[pltpu.VMEM(leaf.shape, leaf.dtype) for leaf in state_shape] if last_call else [],
        compiler_params=pltpu.CompilerParams(vmem_limit_bytes=24 * 1024 * 1024),
        cost_estimate=pl.CostEstimate(
            flops=len(plan) * 8 * GROUP * TOK * 1024 * HD,
            bytes_accessed=4 << 20,
            transcendentals=len(plan) * GROUP * TOK * 1024,
        ),
    )(place, query, *slabs, *state)


def project_kernel(place_ref, *refs):
    pieces_ref, weight_ref, columns_ref, partial_ref = refs
    y = place_ref[0]
    for piece in range(NX):
        columns_ref[:, :, piece] = pieces_ref[piece]
    weight = []
    for row in range(NY):
        for core in range(NC):
            block = weight_ref[core, (y + NY - row) % NY]
            weight.append(jnp.concatenate([block[:FEAT], block[FEAT:]], axis=1))
    weight = jnp.concatenate(weight)
    for slab in range(NZ):
        rows = columns_ref[slab].reshape(TOK, NY * NC * FEAT)
        partial_ref[slab] = jnp.dot(rows, weight, preferred_element_type=jnp.float32).astype(jnp.bfloat16)


def project(place, pieces, weight):
    vmem = pl.BlockSpec(memory_space=pltpu.VMEM)
    return pl.pallas_call(
        project_kernel,
        out_shape=(
            jax.ShapeDtypeStruct((NZ, NW, NX, SHARE, NY * NC * FEAT), jnp.bfloat16),
            jax.ShapeDtypeStruct((NZ, TOK, 2 * HD), jnp.bfloat16),
        ),
        in_specs=[pl.BlockSpec(memory_space=pltpu.SMEM)] + [vmem] * 2,
        out_specs=(vmem, vmem),
        compiler_params=pltpu.CompilerParams(vmem_limit_bytes=24 * 1024 * 1024),
        cost_estimate=pl.CostEstimate(
            flops=2 * NZ * TOK * 512 * 256, bytes_accessed=3 << 20, transcendentals=0
        ),
    )(place, pieces, weight)


def pack_kernel(key_ref, value_ref, codes_ref, exponents_ref, own_ref):
    own_ref[0] = key_ref[...]
    own_ref[1] = value_ref[...]
    scale = jnp.exp2(-exponents_ref[...].astype(jnp.float32)) / math.sqrt(D_S)
    weight = (codes_ref[...].astype(jnp.float32) * scale).astype(jnp.bfloat16)
    own_ref[2, :FEAT] = weight[:, :HD]
    own_ref[2, FEAT:] = weight[:, HD:]


def pack(key, value, codes, exponents):
    vmem = pl.BlockSpec(memory_space=pltpu.VMEM)
    return pl.pallas_call(
        pack_kernel,
        out_shape=jax.ShapeDtypeStruct((3, TOK, HD), jnp.bfloat16),
        in_specs=[vmem] * 4,
        out_specs=vmem,
    )(key, value, codes, exponents.reshape(1, -1))


def shift(array, axis, size, step):
    return lax.ppermute(array, axis, [(i, (i + step) % size) for i in range(size)])


def round_z(array):
    pairs = [(i * NC, (i + 1) % NZ * NC) for i in range(NZ)]
    pairs += [(i * NC + 1, (i - 1) % NZ * NC + 1) for i in range(NZ)]
    return lax.ppermute(array, ("z", "c"), pairs)


def per_device(query, key, value, hidden, codes, exponents):
    y, z, c = lax.axis_index("y"), lax.axis_index("z"), lax.axis_index("c")
    w, x = lax.axis_index("w"), lax.axis_index("x")
    place = jnp.stack([y, z, c, w, x])
    after = lax.optimization_barrier

    own = pack(key, value, codes, exponents)
    rows = jnp.stack([own] + [shift(own, "y", NY, step) for step in range(1, NY)])
    both = lax.all_gather(rows, "c", axis=0, tiled=False)
    slab, weight_rows = both[:, :, :2], both[:, :, 2]

    clipped = jnp.clip(hidden, -CLIP, CLIP)
    chunks = (
        clipped.reshape(SHARE, NY, NZ, NC, FEAT).transpose(2, 0, 1, 3, 4).reshape(NZ, SHARE, NY * NC * FEAT)
    )
    swapped = shift(chunks, "w", NW, 1)
    pair = jnp.stack(
        [jnp.where(w == 0, chunks, swapped), jnp.where(w == 0, swapped, chunks)], axis=1
    )

    def slab_in(ref, *path):
        return tuple((ref, path + (core,)) for core in range(NC))

    slab, pair = after((slab, pair))
    near = round_z(slab)
    pair = lax.all_to_all(pair, "z", 0, 0)
    near, pair = after((near, pair))
    far = round_z(near)
    pieces = lax.all_to_all(jnp.broadcast_to(pair[None], (NX,) + pair.shape), "x", 0, 0)
    state = attend(place, query, ((0, slab_in(0)), (1, slab_in(1))), (slab, near), None)

    state, far, pieces = after((state, far, pieces))
    columns, partial = project(place, pieces, weight_rows)
    columns = columns.reshape(NZ * TOK, NY * NC * FEAT)
    partial, state, far = after((partial, state, far))
    received = lax.all_to_all(partial, "z", 0, 0)
    third = round_z(far)
    two_other = shift(jnp.stack([near, far]), "c", NC, 1)
    state = attend(place, query, ((2, slab_in(0)),), (far,), state)

    state, third = after((state, third))
    fourth = round_z(jnp.where(c == 0, third[0], third[1]))
    state = attend(
        place, query, ((3, slab_in(0)), (-1, slab_in(1, 0)), (-2, slab_in(1, 1))), (third, two_other), state
    )

    state, third, fourth, received = after((state, third, fourth, received))
    last_other = shift(jnp.concatenate([third, fourth[None]]), "c", NC, 1)
    projected = jnp.sum(received.astype(jnp.float32), axis=0)
    student = lax.all_to_all(
        projected.astype(jnp.bfloat16).reshape(NW * NX, SHARE, -1), HEAD, 0, 0
    )
    teacher_context, target = attend(
        place,
        query,
        ((-3, slab_in(1)), (4, ((0, ()), (1, (NC,))))),
        (fourth, last_other),
        state,
        last_call=True,
    )

    target, student = after((target, student))
    student_out = student.transpose(1, 0, 2).reshape(SHARE, -1)
    residue = (projected - target).astype(jnp.bfloat16)
    residue = lax.all_to_all(jnp.broadcast_to(residue[None], (NZ,) + residue.shape), "z", 0, 0)
    grad = lax.dot_general(
        columns,
        residue.reshape(NZ * TOK, -1),
        (((0,), (0,)), ((), ())),
        preferred_element_type=jnp.float32,
    ) * (1.0 / math.sqrt(NY * NZ * NC * TOK))
    grad = grad.astype(jnp.bfloat16).reshape(NY * NC, FEAT, -1)
    weight_grad = jnp.sum(lax.all_to_all(grad, ("y", "c"), 0, 0).astype(jnp.float32), axis=0)
    return teacher_context, student_out, weight_grad


def solution(mesh):
    fine = Mesh(mesh.devices.reshape(NY, NZ, NC, NW, NX), ("y", "z", "c", "w", "x"))
    return jax.shard_map(
        per_device,
        mesh=fine,
        in_specs=(
            P(CTX, HEAD),
            P(CTX, HEAD),
            P(CTX, HEAD),
            P(CTX + HEAD, None),
            P(CTX, HEAD),
            P(HEAD),
        ),
        out_specs=(P(CTX, HEAD), P(CTX + HEAD, None), P(CTX, HEAD)),
        check_vma=False,
    )
```
